32 devices in a mesh: dp: 32 (over z, y, x, core).
Axes of the slice: x: 2, y: 2, z: 4, core: 2. Of those that a mesh axis runs over, the one named last changes fastest.
Arguments:
- tokens: bfloat16 [8192, 896], P('dp'), may hold values from -6 to 6
- attn_weights: bfloat16 [2048, 896], P('dp'), may hold values from -2 to 2
- mlp_weights: bfloat16 [4864, 3, 896], P('dp'), may hold values from -0.1875 to 0.1875
- norm_gains: bfloat16 [2, 896], replicated, may hold values from 0.5 to 1.5
- qkv_bias: bfloat16 [1152], replicated, may hold values from -3 to 3
- seq_lengths: int32 [32, 8], P('dp'), may hold values from 0 to 256, as said below
- cotangent: bfloat16 [8192, 896], P('dp'), may hold values from -6 to 6
Outputs:
- layer_out: bfloat16 [8192, 896], P('dp')
- grad_tokens: float32 [8192, 896], P('dp')
- grad_attn: float32 [2048, 896], P('dp')
- grad_mlp: float32 [4864, 3, 896], P('dp')
- grad_gains: float32 [2, 896], replicated
- grad_bias: float32 [1152], replicated
The draws below stay inside these ranges and needn't reach their ends.
Inputs may be any that keep to these rules, and one draw needn't show every extreme that they name: `seq_lengths`: the lengths of one device add up to at most 256 and at least 128; its slots beyond that sum are padding. In every draw one device holds a single sequence of exactly 256 tokens.
All inputs are finite; a program needn't handle non-finite values.
Results may differ from the reference program's by a relative error of at most 0.011.
Values may be sent and summed in bfloat16 or wider, within the bound.
A program may use at most 256 MiB of HBM per device.

```python
import jax
import jax.numpy as jnp
from jax import lax

HEADS = 14
KV_HEADS = 2
HEAD = 64
FF = 4864
TOK_DEV = 256
SEQS_DEV = 8
D = 896
GROUP = 7
QKV = 1152
ATT_ROWS = 2048
TOKENS = 8192
N_DP = 32


output_gain = 6.0


def draw_attn_weights(key, part):
    key = jax.random.fold_in(key, 7)
    base = jnp.clip(jax.random.normal(key, (ATT_ROWS, D), jnp.float32), -3.0, 3.0)
    row_index = jnp.arange(ATT_ROWS)
    factor = jnp.where(row_index < QKV, 1.0, output_gain)
    return (base * factor[:, None] * D ** (-0.5)).astype(jnp.bfloat16)


def draw_seq_lengths(key, part):
    key = jax.random.fold_in(key, 11)
    fill_key, share_key, pick_key = jax.random.split(key, 3)
    filled = jax.random.randint(fill_key, (N_DP, 1), TOK_DEV // 2, TOK_DEV + 1)
    shares = jax.random.randint(share_key, (N_DP, SEQS_DEV), 1, 17)
    spare_tokens = filled - SEQS_DEV
    pieces = 1 + spare_tokens * shares // jnp.sum(shares, axis=1, keepdims=True)
    leftover = filled[:, 0] - jnp.sum(pieces, axis=1)
    first_column = (jnp.arange(SEQS_DEV) == 0).astype(jnp.int32)
    pieces = pieces + leftover[:, None] * first_column[None, :]
    chosen = jax.random.randint(pick_key, (), 0, N_DP)
    whole_row = first_column * TOK_DEV
    picked = jnp.arange(N_DP)[:, None] == chosen
    return jnp.where(picked, whole_row[None, :], pieces).astype(jnp.int32)


def block_scale(own_key, dims, shards, smallest, largest):
    def one(dim, shards_of):
        heights = jax.random.uniform(jax.random.fold_in(jax.random.fold_in(own_key, 6), dim), (shards_of,), jnp.float32, smallest / len(shards), largest / len(shards))
        return jnp.repeat(jnp.exp(heights), dims[dim] // shards_of).reshape((-1,) + (1,) * (len(dims) - dim - 1))

    level = one(*shards[0])
    for cut in shards[1:]:
        level = level * one(*cut)
    return level


def bell_draw(own_key, dims, deviation, limit, cuts=(), kind=jnp.bfloat16):
    values = deviation * jax.random.normal(own_key, dims, jnp.float32)
    if cuts:
        values = values * block_scale(own_key, dims, cuts, -0.22, 0.18)
    return jnp.clip(values, -limit, limit).astype(kind)


def setup_inputs(seed: int = 0) -> dict:
    keys = jax.random.split(jax.random.key(seed), 8)
    return {
        "tokens": bell_draw(keys[0], (TOKENS, D), 1.0, 6.0, ((0, 32),)),
        "attn_weights": draw_attn_weights(jax.random.fold_in(keys[7], 71), 0),
        "mlp_weights": bell_draw(keys[2], (FF, 3, D), D ** -0.5, 0.1875, ((0, 32),)),
        "norm_gains": jnp.clip(1.0 + 0.1 * jax.random.normal(keys[3], (2, D), jnp.float32), 0.5, 1.5).astype(jnp.bfloat16),
        "qkv_bias": bell_draw(keys[4], (QKV,), 0.5, 3.0),
        "seq_lengths": draw_seq_lengths(jax.random.fold_in(keys[7], 71), 0),
        "cotangent": bell_draw(keys[6], (TOKENS, D), 1.0, 6.0, ((0, 32),)),
    }


epsilon = 1e-06
rope_base = 1000000.0
neg_fill = -1e+30

@jax.custom_vjp
def low(v):
    return lax.optimization_barrier(v.astype(jnp.bfloat16)).astype(jnp.float32)

@jax.custom_vjp
def low_back(v):
    return v

def low_keep(v):
    return (low(v), None)

def low_pass(kept, grad):
    return (grad,)

def back_keep(v):
    return (v, None)

def back_low(kept, grad):
    return (low(grad),)
low.defvjp(low_keep, low_pass)
low_back.defvjp(back_keep, back_low)

def matmul(left, right):
    return jnp.dot(left, right, precision=lax.Precision.HIGHEST, preferred_element_type=jnp.float32)

def layout(lengths):
    slot_index = jnp.arange(TOK_DEV, dtype=jnp.int32)
    lengths = lengths.astype(jnp.int32)
    seq_ends = jnp.cumsum(lengths).astype(jnp.int32)
    seq_starts = (seq_ends - lengths).astype(jnp.int32)
    filled = seq_ends[SEQS_DEV - 1]
    segment = lax.optimization_barrier(jnp.sum((slot_index[:, None] >= seq_ends[None, :]).astype(jnp.int32), axis=1)).astype(jnp.int32)
    starts_all = jnp.concatenate([seq_starts, filled[None]]).astype(jnp.int32)
    which = segment[:, None] == jnp.arange(SEQS_DEV + 1, dtype=jnp.int32)[None, :]
    start_of = lax.optimization_barrier(jnp.sum(jnp.where(which, starts_all[None, :], 0), axis=1)).astype(jnp.int32)
    position = (slot_index - start_of).astype(jnp.int32)
    live = slot_index < filled
    return (segment, position, live)

def half_turn(heads):
    middle = heads.shape[-1] // 2
    return jnp.concatenate([-heads[..., middle:], heads[..., :middle]], axis=-1)

def rope_tables(position):
    index = jnp.arange(HEAD // 2, dtype=jnp.float32)
    freqs = rope_base ** (-2.0 * index / HEAD)
    angles = position.astype(jnp.float32)[:, None] * freqs[None, :]
    angles = jnp.concatenate([angles, angles], axis=1)
    return (jnp.cos(angles), jnp.sin(angles))

def normalize(values, gain):
    return values * lax.rsqrt(lax.optimization_barrier(jnp.mean(values * values, axis=-1, keepdims=True)) + epsilon) * gain[None, :]

def forward(inputs, attention, feedfwd, gains, biases, segment, position):
    num_rows = inputs.shape[0]
    kv_width = KV_HEADS * HEAD
    normed = low(normalize(inputs, gains[0]))
    projected = low_back(matmul(normed, attention[:QKV].T) + biases[None, :])
    cosine, sine_table = rope_tables(position)
    cos_three = cosine[:, None, :]
    sin_three = sine_table[:, None, :]
    query = projected[:, :D].reshape(num_rows, HEADS, HEAD)
    key_heads = projected[:, D:D + kv_width].reshape(num_rows, KV_HEADS, HEAD)
    value_heads = projected[:, D + kv_width:].reshape(num_rows, KV_HEADS, HEAD)
    query = low(query * cos_three + half_turn(query) * sin_three).reshape(num_rows, KV_HEADS, GROUP, HEAD)
    key_heads = low(key_heads * cos_three + half_turn(key_heads) * sin_three)
    value_heads = low(value_heads)
    raw_scores = low_back(jnp.einsum('qkgh,skh->kgqs', query, key_heads, precision=lax.Precision.HIGHEST))
    slot_index = jnp.arange(num_rows, dtype=jnp.int32)
    allowed = (segment[:, None] == segment[None, :]) & (slot_index[None, :] <= slot_index[:, None])
    scores = jnp.where(allowed[None, None], raw_scores * HEAD ** (-0.5), neg_fill)
    row_peak = lax.optimization_barrier(jnp.max(scores, axis=-1, keepdims=True))
    exponent = jnp.exp(scores - row_peak)
    probs = low(exponent / lax.optimization_barrier(jnp.sum(exponent, axis=-1, keepdims=True)))
    mixed_heads = jnp.einsum('kgqs,skh->qkgh', probs, value_heads, precision=lax.Precision.HIGHEST)
    attended = low(low_back(mixed_heads.reshape(num_rows, D)))
    hidden = inputs + low_back(matmul(attended, attention[QKV:].T))
    normed_two = low(normalize(hidden, gains[1]))
    gate_proj = low_back(matmul(normed_two, feedfwd[:, 0, :].T))
    up_proj = low_back(matmul(normed_two, feedfwd[:, 1, :].T))
    active = low(jax.nn.silu(gate_proj) * up_proj)
    return hidden + low_back(matmul(active, feedfwd[:, 2, :]))

def reference(tokens, attn_weights, mlp_weights, norm_gains, qkv_bias, seq_lengths, cotangent):
    attention = attn_weights.astype(jnp.float32)
    feedfwd = mlp_weights.astype(jnp.float32)
    gains = norm_gains.astype(jnp.float32)
    biases = qkv_bias.astype(jnp.float32)
    token_blocks = tokens.reshape(N_DP, TOK_DEV, D)
    cot_blocks = cotangent.reshape(N_DP, TOK_DEV, D)

    def device_block(running, item):
        token_block, cot_block, length_row = item
        segment, position, live = layout(length_row)

        def layer(inputs, att_full, mlp_full, gain_rows, bias_row):
            return forward(inputs, att_full, mlp_full, gain_rows, bias_row, segment, position)
        result, pullback = jax.vjp(layer, token_block.astype(jnp.float32), attention, feedfwd, gains, biases)
        upstream = cot_block.astype(jnp.float32) * live.astype(jnp.float32)[:, None]
        gradients = pullback(upstream)
        running = tuple((earlier + gradient for earlier, gradient in zip(running, gradients[1:])))
        return (running, (result.astype(jnp.bfloat16), gradients[0]))
    initial = (jnp.zeros((ATT_ROWS, D), jnp.float32), jnp.zeros((FF, 3, D), jnp.float32), jnp.zeros((2, D), jnp.float32), jnp.zeros((QKV,), jnp.float32))
    running, (outputs, input_grads) = lax.scan(device_block, initial, (token_blocks, cot_blocks, seq_lengths))
    return (outputs.reshape(TOKENS, D), input_grads.reshape(TOKENS, D), running[0], running[1], running[2], running[3])
```

```python
import jax
import jax.numpy as jnp
from jax import lax
from jax.sharding import PartitionSpec as P

HEADS = 14
KV_HEADS = 2
HEAD = 64
SEQS_DEV = 8
D = 896
GROUP = 7
QKV = 1152


epsilon = 1e-06
rope_base = 1000000.0
neg_fill = -1e30


def layout(lengths, slot_count):
    slot_index = jnp.arange(slot_count, dtype=jnp.int32)
    seq_ends = jnp.cumsum(lengths)
    seq_starts = seq_ends - lengths
    filled = seq_ends[SEQS_DEV - 1]
    segment = jnp.sum((slot_index[:, None] >= seq_ends[None, :]).astype(jnp.int32), axis=1)
    starts_all = jnp.concatenate([seq_starts, filled[None]])
    which = segment[:, None] == jnp.arange(SEQS_DEV + 1, dtype=jnp.int32)[None, :]
    start_of = jnp.sum(jnp.where(which, starts_all[None, :], 0), axis=1)
    position = slot_index - start_of
    live = slot_index < filled
    return (segment, position, live)


def half_turn(heads):
    middle = heads.shape[-1] // 2
    return jnp.concatenate([-heads[..., middle:], heads[..., :middle]], axis=-1)


def rope_tables(position):
    index = jnp.arange(HEAD // 2, dtype=jnp.float32)
    freqs = rope_base ** (-2.0 * index / HEAD)
    angles = position.astype(jnp.float32)[:, None] * freqs[None, :]
    angles = jnp.concatenate([angles, angles], axis=1)
    return (jnp.cos(angles), jnp.sin(angles))


def rotate(heads, cosine, sine_table):
    return heads * cosine[:, None, :] + half_turn(heads) * sine_table[:, None, :]


def unrotate(grads, cosine, sine_table):
    return grads * cosine[:, None, :] - half_turn(grads * sine_table[:, None, :])


def normalize(values, gain):
    inv_rms = lax.rsqrt(jnp.mean(values * values, axis=-1, keepdims=True) + epsilon)
    return (values * inv_rms * gain[None, :], inv_rms)


def norm_backward(values, gain, inv_rms, upstream):
    scaled = gain[None, :] * upstream
    gain_grad = jnp.sum(upstream * values * inv_rms, axis=0)
    input_grad = inv_rms * scaled - values * inv_rms**3 * jnp.mean(
        scaled * values, axis=-1, keepdims=True
    )
    return (input_grad, gain_grad)


def contract_last(left, right):
    return lax.dot_general(
        left, right, (((1,), (1,)), ((), ())), preferred_element_type=jnp.float32
    )


def contract_first(left, right):
    return lax.dot_general(
        left, right, (((0,), (0,)), ((), ())), preferred_element_type=jnp.float32
    )


def plain_dot(left, right):
    return jnp.dot(left, right, preferred_element_type=jnp.float32)


def bits_of(size):
    return size.bit_length() - 1


def swap(value, size, bit):
    return lax.ppermute(value, "dp", [(i, i ^ (1 << bit)) for i in range(size)])


def scatter_sum(parts, order, size, index):
    held = sorted(order, reverse=True)
    last = order[-1]
    for bit in order:
        axis = held.index(bit)
        mine = (index >> bit) & 1
        away = lax.dynamic_index_in_dim(parts, 1 - mine, axis, keepdims=False)
        kept = lax.dynamic_index_in_dim(parts, mine, axis, keepdims=False)
        come = swap(away, size, bit)
        total = kept.astype(jnp.float32) + come.astype(jnp.float32)
        parts = total if bit == last else total.astype(jnp.bfloat16)
        held.remove(bit)
    return parts


def orders_of(size):
    bits = list(range(1, bits_of(size)))
    third = max(1, len(bits) // 4)
    if len(bits) < 3:
        return (bits, bits, bits)
    x_bits, y_bits = bits[:third], bits[third : 2 * third]
    z_bits = bits[2 * third :]
    return (x_bits + y_bits + z_bits, y_bits + x_bits + z_bits, z_bits + x_bits + y_bits)


def total_over(value, size):
    for bit in range(bits_of(size)):
        value = value + swap(value, size, bit)
    return value


def split_rows(value, count, rows):
    return value.reshape((2,) * bits_of(count) + (rows, value.shape[-1]))


def body(tokens, attn_weights, mlp_weights, norm_gains, qkv_bias, seq_lengths, cotangent):
    size = lax.axis_size("dp")
    index = lax.axis_index("dp")
    core = index & 1
    half = size // 2
    same_core = [list(range(0, size, 2)), list(range(1, size, 2))]
    orders = orders_of(size)
    num_rows = tokens.shape[0]
    attn_owned = attn_weights.shape[0]
    mlp_owned = mlp_weights.shape[0]
    kv_width = KV_HEADS * HEAD

    attn_half = lax.all_gather(attn_weights, "dp", axis=0, axis_index_groups=same_core)
    mlp_flat = mlp_weights.reshape(mlp_owned, 3 * D)
    feedfwd = lax.all_gather(
        mlp_flat, "dp", axis=0, axis_index_groups=same_core, tiled=True
    )
    attn_other = swap(attn_half, size, 0)
    attention = jnp.stack(
        [jnp.where(core == 0, attn_half, attn_other), jnp.where(core == 0, attn_other, attn_half)],
        axis=1,
    ).reshape(size * attn_owned, D)
    w_gate, w_up, w_down = feedfwd[:, :D], feedfwd[:, D : 2 * D], feedfwd[:, 2 * D :]

    segment, position, live = layout(seq_lengths[0], num_rows)
    slot_index = jnp.arange(num_rows, dtype=jnp.int32)
    gains = norm_gains.astype(jnp.float32)
    biases = qkv_bias.astype(jnp.float32)
    inputs = tokens.astype(jnp.float32)
    upstream = cotangent.astype(jnp.float32) * live.astype(jnp.float32)[:, None]
    upstream_low = upstream.astype(jnp.bfloat16)
    upstream_two = jnp.concatenate([upstream_low, swap(upstream_low, size, 0)], axis=0)

    normed_one, inv_one = normalize(inputs, gains[0])
    normed_low = normed_one.astype(jnp.bfloat16)
    projected = contract_last(normed_low, attention[:QKV]) + biases[None, :]
    cosine, sine_table = rope_tables(position)
    query_low = rotate(projected[:, :D].reshape(num_rows, HEADS, HEAD), cosine, sine_table).astype(
        jnp.bfloat16
    )
    key_low = rotate(
        projected[:, D : D + kv_width].reshape(num_rows, KV_HEADS, HEAD), cosine, sine_table
    ).astype(jnp.bfloat16)
    value_low = projected[:, D + kv_width :].reshape(num_rows, KV_HEADS, HEAD).astype(jnp.bfloat16)
    query = query_low.reshape(num_rows, KV_HEADS, GROUP, HEAD)
    allowed = (segment[:, None] == segment[None, :]) & (slot_index[None, :] <= slot_index[:, None])
    raw_scores = jnp.einsum("qkgh,skh->kgqs", query, key_low, preferred_element_type=jnp.float32)
    scores = jnp.where(allowed[None, None], raw_scores * HEAD ** (-0.5), neg_fill)
    row_peak = jnp.max(scores, axis=-1, keepdims=True)
    exponent = jnp.exp(scores - row_peak)
    row_total = jnp.sum(exponent, axis=-1, keepdims=True)
    probs = exponent / row_total
    probs_low = probs.astype(jnp.bfloat16)
    mixed_heads = jnp.einsum(
        "kgqs,skh->qkgh", probs_low, value_low, preferred_element_type=jnp.float32
    )
    attended_low = mixed_heads.reshape(num_rows, D).astype(jnp.bfloat16)
    hidden = inputs + contract_last(attended_low, attention[QKV:])
    normed_two, inv_two = normalize(hidden, gains[1])
    normed_two_low = normed_two.astype(jnp.bfloat16)

    normed_pair = jnp.concatenate([normed_two_low, swap(normed_two_low, size, 0)], axis=0)
    gate_proj = contract_last(normed_pair, w_gate)
    up_proj = contract_last(normed_pair, w_up)
    gate_sigmoid = jax.nn.sigmoid(gate_proj)
    active_low = (gate_proj * gate_sigmoid * up_proj).astype(jnp.bfloat16)
    grad_active = contract_last(upstream_two, w_down)
    grad_gate_low = (
        grad_active * up_proj * gate_sigmoid * (1.0 + gate_proj * (1.0 - gate_sigmoid))
    ).astype(jnp.bfloat16)
    grad_up_low = (grad_active * gate_proj * gate_sigmoid).astype(jnp.bfloat16)
    back_pair = plain_dot(grad_gate_low, w_gate) + plain_dot(grad_up_low, w_up)
    grad_normed_two = back_pair[:num_rows] + swap(back_pair[num_rows:], size, 0)
    down_pair = plain_dot(active_low, w_down)
    layer_out = (hidden + (down_pair[:num_rows] + swap(down_pair[num_rows:], size, 0))).astype(
        jnp.bfloat16
    )

    def weight_sum(left, right, order):
        term = contract_first(left, right).astype(jnp.bfloat16)
        return scatter_sum(split_rows(term, half, mlp_owned), order, size, index)

    sum_down = weight_sum(active_low, upstream_two, orders[2])
    sum_gate = weight_sum(grad_gate_low, normed_pair, orders[0])
    sum_up = weight_sum(grad_up_low, normed_pair, orders[1])

    grad_mid, grad_gain_two = norm_backward(hidden, gains[1], inv_two, grad_normed_two)
    grad_hidden = upstream + grad_mid
    grad_hidden_low = grad_hidden.astype(jnp.bfloat16)
    grad_out_proj = contract_first(grad_hidden_low, attended_low).astype(jnp.bfloat16)
    grad_attended_low = plain_dot(grad_hidden_low, attention[QKV:]).astype(jnp.bfloat16)
    grad_part = grad_attended_low.reshape(num_rows, KV_HEADS, GROUP, HEAD)
    value_grad = jnp.einsum(
        "kgqs,qkgh->skh", probs_low, grad_part, preferred_element_type=jnp.float32
    )
    grad_probs = jnp.einsum(
        "qkgh,skh->kgqs", grad_part, value_low, preferred_element_type=jnp.float32
    )
    row_inner = jnp.sum(probs * grad_probs, axis=-1, keepdims=True)
    score_grad_low = (probs * (grad_probs - row_inner) * HEAD ** (-0.5)).astype(jnp.bfloat16)
    query_grad = jnp.einsum(
        "kgqs,skh->qkgh", score_grad_low, key_low, preferred_element_type=jnp.float32
    )
    key_grad = jnp.einsum(
        "kgqs,qkgh->skh", score_grad_low, query, preferred_element_type=jnp.float32
    )
    query_pre = unrotate(query_grad.reshape(num_rows, HEADS, HEAD), cosine, sine_table)
    key_pre = unrotate(key_grad, cosine, sine_table)
    grad_qkv_low = jnp.concatenate(
        [
            query_pre.reshape(num_rows, D),
            key_pre.reshape(num_rows, kv_width),
            value_grad.reshape(num_rows, kv_width),
        ],
        axis=1,
    ).astype(jnp.bfloat16)
    grad_bias_term = jnp.sum(grad_qkv_low, axis=0, dtype=jnp.float32)
    grad_qkv_weights = contract_first(grad_qkv_low, normed_low).astype(jnp.bfloat16)
    grad_normed_one = plain_dot(grad_qkv_low, attention[:QKV])
    grad_input_mid, grad_gain_one = norm_backward(inputs, gains[0], inv_one, grad_normed_one)
    grad_tokens = grad_hidden + grad_input_mid

    attn_term = jnp.concatenate([grad_qkv_weights, grad_out_proj], axis=0)
    edges = (0, 384, 640, D)
    grad_attn = jnp.concatenate(
        [
            scatter_sum(
                split_rows(attn_term[:, left:right], size, attn_owned), [0] + order, size, index
            )
            for left, right, order in zip(edges[:-1], edges[1:], orders)
        ],
        axis=1,
    )
    grad_mlp = jnp.stack([sum_gate, sum_up, sum_down], axis=1)
    small = total_over(jnp.concatenate([grad_gain_one, grad_gain_two, grad_bias_term]), size)
    grad_gains = small[: 2 * D].reshape(2, D)
    return (layer_out, grad_tokens, grad_attn, grad_mlp, grad_gains, small[2 * D :])


def solution(mesh):
    placed = (
        P("dp", None),
        P("dp", None),
        P("dp", None, None),
        P(),
        P(),
        P("dp", None),
        P("dp", None),
    )
    return jax.shard_map(
        body,
        mesh=mesh,
        in_specs=placed,
        out_specs=(P("dp", None), P("dp", None), P("dp", None), P("dp", None, None), P(), P()),
        check_vma=False,
    )
```

```python
import jax
import jax.numpy as jnp
from jax import lax
from jax.sharding import PartitionSpec as P

HEADS = 14
KV_HEADS = 2
HEAD = 64
SEQS_DEV = 8
D = 896
GROUP = 7
QKV = 1152


epsilon = 1e-06
rope_base = 1000000.0
neg_fill = -1e30


def layout(lengths, slot_count):
    slot_index = jnp.arange(slot_count, dtype=jnp.int32)
    seq_ends = jnp.cumsum(lengths)
    seq_starts = seq_ends - lengths
    filled = seq_ends[SEQS_DEV - 1]
    segment = jnp.sum((slot_index[:, None] >= seq_ends[None, :]).astype(jnp.int32), axis=1)
    starts_all = jnp.concatenate([seq_starts, filled[None]])
    which = segment[:, None] == jnp.arange(SEQS_DEV + 1, dtype=jnp.int32)[None, :]
    start_of = jnp.sum(jnp.where(which, starts_all[None, :], 0), axis=1)
    position = slot_index - start_of
    live = slot_index < filled
    return (segment, position, live)


def half_turn(heads):
    middle = heads.shape[-1] // 2
    return jnp.concatenate([-heads[..., middle:], heads[..., :middle]], axis=-1)


def rope_tables(position):
    index = jnp.arange(HEAD // 2, dtype=jnp.float32)
    freqs = rope_base ** (-2.0 * index / HEAD)
    angles = position.astype(jnp.float32)[:, None] * freqs[None, :]
    angles = jnp.concatenate([angles, angles], axis=1)
    return (jnp.cos(angles), jnp.sin(angles))


def rotate(heads, cosine, sine_table):
    return heads * cosine[:, None, :] + half_turn(heads) * sine_table[:, None, :]


def unrotate(grads, cosine, sine_table):
    return grads * cosine[:, None, :] - half_turn(grads * sine_table[:, None, :])


def normalize(values, gain):
    inv_rms = lax.rsqrt(jnp.mean(values * values, axis=-1, keepdims=True) + epsilon)
    return (values * inv_rms * gain[None, :], inv_rms)


def norm_backward(values, gain, inv_rms, upstream):
    scaled = gain[None, :] * upstream
    gain_grad = jnp.sum(upstream * values * inv_rms, axis=0)
    input_grad = inv_rms * scaled - values * inv_rms**3 * jnp.mean(
        scaled * values, axis=-1, keepdims=True
    )
    return (input_grad, gain_grad)


def contract_last(left, right):
    return lax.dot_general(
        left, right, (((1,), (1,)), ((), ())), preferred_element_type=jnp.float32
    )


def contract_first(left, right):
    return lax.dot_general(
        left, right, (((0,), (0,)), ((), ())), preferred_element_type=jnp.float32
    )


def plain_dot(left, right):
    return jnp.dot(left, right, preferred_element_type=jnp.float32)


def bits_of(size):
    return size.bit_length() - 1


def swap(value, size, bit):
    return lax.ppermute(value, "dp", [(i, i ^ (1 << bit)) for i in range(size)])


def orders_of(size):
    bits = list(range(1, bits_of(size)))
    near, far = bits[:3], bits[3:]
    return tuple(near[i:] + near[:i] + far for i in range(3))


def start_together(values):
    return list(lax.optimization_barrier(tuple(values)))


def take(value, axis, which):
    return lax.index_in_dim(value, which, axis, keepdims=False)


def add_low(kept, come, last):
    total = kept.astype(jnp.float32) + come.astype(jnp.float32)
    return total if last else total.astype(jnp.bfloat16)


def split_rows(value, count, rows):
    return value.reshape((2,) * bits_of(count) + (rows, value.shape[-1]))


def body(tokens, attn_weights, mlp_weights, norm_gains, qkv_bias, seq_lengths, cotangent):
    size = lax.axis_size("dp")
    index = lax.axis_index("dp")
    core = index & 1
    half = size // 2
    same_core = [list(range(0, size, 2)), list(range(1, size, 2))]
    orders = orders_of(size)
    num_rows = tokens.shape[0]
    attn_owned = attn_weights.shape[0]
    mlp_owned = mlp_weights.shape[0]
    kv_width = KV_HEADS * HEAD

    attn_half = lax.all_gather(attn_weights, "dp", axis=0, axis_index_groups=same_core)
    pieces = [mlp_weights[:, i, :] for i in range(3)]
    held = [[], [], []]
    steps = len(orders[0])
    for step in range(steps):
        if step:
            pieces = start_together(pieces)
        if step == steps - 1:
            attn_half, *pieces = start_together([attn_half] + pieces)
        for i in range(3):
            bit = orders[i][steps - 1 - step]
            come = swap(pieces[i], size, bit)
            held[i] = sorted(held[i] + [bit], reverse=True)
            pieces[i] = jnp.stack([pieces[i], come], axis=held[i].index(bit))
    w_gate, w_up, w_down = [piece.reshape(half * mlp_owned, D) for piece in pieces]
    attn_other = swap(attn_half, size, 0)
    attention = jnp.stack(
        [jnp.where(core == 0, attn_half, attn_other), jnp.where(core == 0, attn_other, attn_half)],
        axis=1,
    ).reshape(size * attn_owned, D)

    segment, position, live = layout(seq_lengths[0], num_rows)
    slot_index = jnp.arange(num_rows, dtype=jnp.int32)
    gains = norm_gains.astype(jnp.float32)
    biases = qkv_bias.astype(jnp.float32)
    inputs = tokens.astype(jnp.float32)
    upstream = cotangent.astype(jnp.float32) * live.astype(jnp.float32)[:, None]
    upstream_low = upstream.astype(jnp.bfloat16)
    upstream_two = jnp.concatenate([upstream_low, swap(upstream_low, size, 0)], axis=0)

    normed_one, inv_one = normalize(inputs, gains[0])
    normed_low = normed_one.astype(jnp.bfloat16)
    projected = contract_last(normed_low, attention[:QKV]) + biases[None, :]
    cosine, sine_table = rope_tables(position)
    query_low = rotate(projected[:, :D].reshape(num_rows, HEADS, HEAD), cosine, sine_table).astype(
        jnp.bfloat16
    )
    key_low = rotate(
        projected[:, D : D + kv_width].reshape(num_rows, KV_HEADS, HEAD), cosine, sine_table
    ).astype(jnp.bfloat16)
    value_low = projected[:, D + kv_width :].reshape(num_rows, KV_HEADS, HEAD).astype(jnp.bfloat16)
    query = query_low.reshape(num_rows, KV_HEADS, GROUP, HEAD)
    allowed = (segment[:, None] == segment[None, :]) & (slot_index[None, :] <= slot_index[:, None])
    raw_scores = jnp.einsum("qkgh,skh->kgqs", query, key_low, preferred_element_type=jnp.float32)
    scores = jnp.where(allowed[None, None], raw_scores * HEAD ** (-0.5), neg_fill)
    row_peak = jnp.max(scores, axis=-1, keepdims=True)
    exponent = jnp.exp(scores - row_peak)
    row_total = jnp.sum(exponent, axis=-1, keepdims=True)
    probs = exponent / row_total
    probs_low = probs.astype(jnp.bfloat16)
    mixed_heads = jnp.einsum(
        "kgqs,skh->qkgh", probs_low, value_low, preferred_element_type=jnp.float32
    )
    attended_low = mixed_heads.reshape(num_rows, D).astype(jnp.bfloat16)
    hidden = inputs + contract_last(attended_low, attention[QKV:])
    normed_two, inv_two = normalize(hidden, gains[1])
    normed_two_low = normed_two.astype(jnp.bfloat16)

    normed_pair = jnp.concatenate([normed_two_low, swap(normed_two_low, size, 0)], axis=0)
    gate_proj = contract_last(normed_pair, w_gate)
    up_proj = contract_last(normed_pair, w_up)
    gate_sigmoid = jax.nn.sigmoid(gate_proj)
    active_low = (gate_proj * gate_sigmoid * up_proj).astype(jnp.bfloat16)
    grad_active = contract_last(upstream_two, w_down)
    grad_gate_low = (
        grad_active * up_proj * gate_sigmoid * (1.0 + gate_proj * (1.0 - gate_sigmoid))
    ).astype(jnp.bfloat16)
    grad_up_low = (grad_active * gate_proj * gate_sigmoid).astype(jnp.bfloat16)
    back_pair = plain_dot(grad_gate_low, w_gate) + plain_dot(grad_up_low, w_up)
    grad_normed_two = back_pair[:num_rows] + swap(back_pair[num_rows:], size, 0)
    down_pair = plain_dot(active_low, w_down)
    layer_out = (hidden + (down_pair[:num_rows] + swap(down_pair[num_rows:], size, 0))).astype(
        jnp.bfloat16
    )

    all_bits = list(range(bits_of(size) - 1, 0, -1))
    mlp_held = [list(all_bits) for _ in range(3)]
    mlp_parts = [
        split_rows(contract_first(left, right).astype(jnp.bfloat16), half, mlp_owned)
        for left, right in (
            (grad_gate_low, normed_pair),
            (grad_up_low, normed_pair),
            (active_low, upstream_two),
        )
    ]

    def mlp_sends(step):
        return [
            take(mlp_parts[i], mlp_held[i].index(orders[i][step]), 1) for i in range(3)
        ]

    def mlp_receive(step, comes):
        for i in range(3):
            bit = orders[i][step]
            kept = take(mlp_parts[i], mlp_held[i].index(bit), 0)
            mlp_held[i].remove(bit)
            mlp_parts[i] = add_low(kept, comes[i], step == steps - 1)

    first_comes = [
        swap(away, size, orders[i][0]) for i, away in enumerate(mlp_sends(0))
    ]

    grad_mid, grad_gain_two = norm_backward(hidden, gains[1], inv_two, grad_normed_two)
    grad_hidden = upstream + grad_mid
    grad_hidden_low = grad_hidden.astype(jnp.bfloat16)
    grad_out_proj = contract_first(grad_hidden_low, attended_low).astype(jnp.bfloat16)
    grad_attended_low = plain_dot(grad_hidden_low, attention[QKV:]).astype(jnp.bfloat16)
    grad_part = grad_attended_low.reshape(num_rows, KV_HEADS, GROUP, HEAD)
    value_grad = jnp.einsum(
        "kgqs,qkgh->skh", probs_low, grad_part, preferred_element_type=jnp.float32
    )
    grad_probs = jnp.einsum(
        "qkgh,skh->kgqs", grad_part, value_low, preferred_element_type=jnp.float32
    )
    row_inner = jnp.sum(probs * grad_probs, axis=-1, keepdims=True)
    score_grad_low = (probs * (grad_probs - row_inner) * HEAD ** (-0.5)).astype(jnp.bfloat16)
    query_grad = jnp.einsum(
        "kgqs,skh->qkgh", score_grad_low, key_low, preferred_element_type=jnp.float32
    )
    key_grad = jnp.einsum(
        "kgqs,qkgh->skh", score_grad_low, query, preferred_element_type=jnp.float32
    )
    query_pre = unrotate(query_grad.reshape(num_rows, HEADS, HEAD), cosine, sine_table)
    key_pre = unrotate(key_grad, cosine, sine_table)
    grad_qkv_low = jnp.concatenate(
        [
            query_pre.reshape(num_rows, D),
            key_pre.reshape(num_rows, kv_width),
            value_grad.reshape(num_rows, kv_width),
        ],
        axis=1,
    ).astype(jnp.bfloat16)
    grad_bias_term = jnp.sum(grad_qkv_low, axis=0, dtype=jnp.float32)
    grad_qkv_weights = contract_first(grad_qkv_low, normed_low).astype(jnp.bfloat16)
    grad_normed_one = plain_dot(grad_qkv_low, attention[:QKV])
    grad_input_mid, grad_gain_one = norm_backward(inputs, gains[0], inv_one, grad_normed_one)
    grad_tokens = grad_hidden + grad_input_mid

    attn_term = jnp.concatenate([grad_qkv_weights, grad_out_proj], axis=0)
    edges = (0, 384, 640, D)
    attn_parts = [
        split_rows(attn_term[:, left:right], size, attn_owned)
        for left, right in zip(edges[:-1], edges[1:])
    ]
    attn_orders = [[0] + order for order in orders]
    attn_held = [list(all_bits) + [0] for _ in range(3)]
    small = jnp.concatenate([grad_gain_one, grad_gain_two, grad_bias_term])
    mlp_receive(0, first_comes)
    for step in range(steps + 1):
        sends, keeps = [], []
        for i in range(3):
            bit = attn_orders[i][step]
            axis = attn_held[i].index(bit)
            mine = (index >> bit) & 1
            sends.append(lax.dynamic_index_in_dim(attn_parts[i], 1 - mine, axis, keepdims=False))
            keeps.append(lax.dynamic_index_in_dim(attn_parts[i], mine, axis, keepdims=False))
            attn_held[i].remove(bit)
        sends.append(small)
        if step + 1 < steps:
            sends += mlp_sends(step + 1)
        sends = start_together(sends)
        small = sends[3]
        comes = [swap(sends[i], size, attn_orders[i][step]) for i in range(3)]
        small = small + swap(small, size, step)
        if step + 1 < steps:
            mlp_receive(
                step + 1,
                [swap(sends[4 + i], size, orders[i][step + 1]) for i in range(3)],
            )
        attn_parts = [add_low(keeps[i], comes[i], step == steps) for i in range(3)]
    grad_attn = jnp.concatenate(attn_parts, axis=1)
    grad_mlp = jnp.stack(mlp_parts, axis=1)
    grad_gains = small[: 2 * D].reshape(2, D)
    return (layer_out, grad_tokens, grad_attn, grad_mlp, grad_gains, small[2 * D :])


def solution(mesh):
    placed = (
        P("dp", None),
        P("dp", None),
        P("dp", None, None),
        P(),
        P(),
        P("dp", None),
        P("dp", None),
    )
    return jax.shard_map(
        body,
        mesh=mesh,
        in_specs=placed,
        out_specs=(P("dp", None), P("dp", None), P("dp", None), P("dp", None, None), P(), P()),
        check_vma=False,
    )
```

```python
import jax
import jax.numpy as jnp
from jax import lax
from jax.sharding import PartitionSpec as P

HEADS = 14
KV_HEADS = 2
HEAD = 64
SEQS_DEV = 8
D = 896
GROUP = 7
QKV = 1152


epsilon = 1e-06
rope_base = 1000000.0
neg_fill = -1e30


def layout(lengths, slot_count):
    slot_index = jnp.arange(slot_count, dtype=jnp.int32)
    seq_ends = jnp.cumsum(lengths)
    seq_starts = seq_ends - lengths
    filled = seq_ends[SEQS_DEV - 1]
    segment = jnp.sum((slot_index[:, None] >= seq_ends[None, :]).astype(jnp.int32), axis=1)
    starts_all = jnp.concatenate([seq_starts, filled[None]])
    which = segment[:, None] == jnp.arange(SEQS_DEV + 1, dtype=jnp.int32)[None, :]
    start_of = jnp.sum(jnp.where(which, starts_all[None, :], 0), axis=1)
    position = slot_index - start_of
    live = slot_index < filled
    return (segment, position, live)


def half_turn(heads):
    middle = heads.shape[-1] // 2
    return jnp.concatenate([-heads[..., middle:], heads[..., :middle]], axis=-1)


def rope_tables(position):
    index = jnp.arange(HEAD // 2, dtype=jnp.float32)
    freqs = rope_base ** (-2.0 * index / HEAD)
    angles = position.astype(jnp.float32)[:, None] * freqs[None, :]
    angles = jnp.concatenate([angles, angles], axis=1)
    return (jnp.cos(angles), jnp.sin(angles))


def rotate(heads, cosine, sine_table):
    return heads * cosine[:, None, :] + half_turn(heads) * sine_table[:, None, :]


def unrotate(grads, cosine, sine_table):
    return grads * cosine[:, None, :] - half_turn(grads * sine_table[:, None, :])


def normalize(values, gain):
    inv_rms = lax.rsqrt(jnp.mean(values * values, axis=-1, keepdims=True) + epsilon)
    return (values * inv_rms * gain[None, :], inv_rms)


def norm_backward(values, gain, inv_rms, upstream):
    scaled = gain[None, :] * upstream
    gain_grad = jnp.sum(upstream * values * inv_rms, axis=0)
    input_grad = inv_rms * scaled - values * inv_rms**3 * jnp.mean(
        scaled * values, axis=-1, keepdims=True
    )
    return (input_grad, gain_grad)


def contract_last(left, right):
    return lax.dot_general(
        left, right, (((1,), (1,)), ((), ())), preferred_element_type=jnp.float32
    )


def contract_first(left, right):
    return lax.dot_general(
        left, right, (((0,), (0,)), ((), ())), preferred_element_type=jnp.float32
    )


def plain_dot(left, right):
    return jnp.dot(left, right, preferred_element_type=jnp.float32)


def bits_of(size):
    return size.bit_length() - 1


def swap(value, size, bit):
    return lax.ppermute(value, "dp", [(i, i ^ (1 << bit)) for i in range(size)])


def orders_of(bits):
    near, far = bits[:3], bits[3:]
    return tuple(near[i:] + near[:i] + far for i in range(3))


def start_together(values):
    return list(lax.optimization_barrier(tuple(values)))


def take(value, axis, which):
    return lax.index_in_dim(value, which, axis, keepdims=False)


def add_low(kept, come, last):
    total = kept.astype(jnp.float32) + come.astype(jnp.float32)
    return total if last else total.astype(jnp.bfloat16)


def split_rows(value, count, rows):
    return value.reshape((2,) * bits_of(count) + (rows, value.shape[-1]))


def body(tokens, attn_weights, mlp_weights, norm_gains, qkv_bias, seq_lengths, cotangent):
    size = lax.axis_size("dp")
    index = lax.axis_index("dp")
    top = bits_of(size) - 1
    quarter = size // 4
    near_bits = list(range(1, top))
    orders = orders_of(near_bits)
    num_rows = tokens.shape[0]
    attn_owned = attn_weights.shape[0]
    mlp_owned = mlp_weights.shape[0]
    kv_width = KV_HEADS * HEAD

    edges = (0, 384, 640, D)
    attn_parts = [attn_weights[:, left:right] for left, right in zip(edges[:-1], edges[1:])]
    attn_held = [[], [], []]
    pieces = [mlp_weights[:, i, :] for i in range(3)]
    held = [[], [], []]
    steps = len(near_bits)

    def widen_attn(step):
        for i in range(3):
            bit = (orders[i] + [top])[steps - step]
            come = swap(attn_parts[i], size, bit)
            first = ((index >> bit) & 1) == 0
            attn_held[i] = sorted(attn_held[i] + [bit], reverse=True)
            attn_parts[i] = jnp.stack(
                [jnp.where(first, attn_parts[i], come), jnp.where(first, come, attn_parts[i])],
                axis=attn_held[i].index(bit),
            )

    def widen_mlp(step):
        for i in range(3):
            bit = orders[i][steps - 1 - step]
            come = swap(pieces[i], size, bit)
            held[i] = sorted(held[i] + [bit], reverse=True)
            pieces[i] = jnp.stack([pieces[i], come], axis=held[i].index(bit))

    attn_parts = start_together(attn_parts)
    widen_attn(0)
    for step in range(steps):
        together = start_together(attn_parts + pieces)
        attn_parts, pieces = together[:3], together[3:]
        widen_attn(step + 1)
        if step < steps - 1:
            widen_mlp(step)
    attn_half = jnp.concatenate(
        [part.reshape(size // 2, attn_owned, part.shape[-1]) for part in attn_parts], axis=2
    )
    attn_half, cotangent, *pieces = start_together([attn_half, cotangent] + pieces)
    attn_other = swap(attn_half, size, 0)
    last_comes = [swap(pieces[i], size, orders[i][0]) for i in range(3)]
    attention = jnp.stack(
        [
            jnp.where(index & 1 == 0, attn_half, attn_other),
            jnp.where(index & 1 == 0, attn_other, attn_half),
        ],
        axis=1,
    ).reshape(size * attn_owned, D)

    def four_blocks(own):
        far = swap(own, size, top)
        return jnp.concatenate([own, swap(own, size, 0), far, swap(far, size, 0)], axis=0)

    def back_to_owner(partial):
        four = partial.reshape(2, 2, num_rows, D)
        pair = four[:, 0] + swap(four[:, 1], size, 0)
        return pair[0] + swap(pair[1].astype(jnp.bfloat16), size, top).astype(jnp.float32)

    segment, position, live = layout(seq_lengths[0], num_rows)
    slot_index = jnp.arange(num_rows, dtype=jnp.int32)
    gains = norm_gains.astype(jnp.float32)
    biases = qkv_bias.astype(jnp.float32)
    inputs = tokens.astype(jnp.float32)
    upstream = cotangent.astype(jnp.float32) * live.astype(jnp.float32)[:, None]
    upstream_low = upstream.astype(jnp.bfloat16)
    upstream_four = four_blocks(upstream_low)

    normed_one, inv_one = normalize(inputs, gains[0])
    normed_low = normed_one.astype(jnp.bfloat16)
    projected = contract_last(normed_low, attention[:QKV]) + biases[None, :]
    cosine, sine_table = rope_tables(position)
    query_low = rotate(projected[:, :D].reshape(num_rows, HEADS, HEAD), cosine, sine_table).astype(
        jnp.bfloat16
    )
    key_low = rotate(
        projected[:, D : D + kv_width].reshape(num_rows, KV_HEADS, HEAD), cosine, sine_table
    ).astype(jnp.bfloat16)
    value_low = projected[:, D + kv_width :].reshape(num_rows, KV_HEADS, HEAD).astype(jnp.bfloat16)
    query_low, *last_comes = start_together([query_low] + last_comes)
    w_gate, w_up, w_down = [
        jnp.stack([pieces[i], last_comes[i]], axis=near_bits[::-1].index(orders[i][0])).reshape(
            quarter * mlp_owned, D
        )
        for i in range(3)
    ]
    query = query_low.reshape(num_rows, KV_HEADS, GROUP, HEAD)
    allowed = (segment[:, None] == segment[None, :]) & (slot_index[None, :] <= slot_index[:, None])
    raw_scores = jnp.einsum("qkgh,skh->kgqs", query, key_low, preferred_element_type=jnp.float32)
    scores = jnp.where(allowed[None, None], raw_scores * HEAD ** (-0.5), neg_fill)
    row_peak = jnp.max(scores, axis=-1, keepdims=True)
    exponent = jnp.exp(scores - row_peak)
    row_total = jnp.sum(exponent, axis=-1, keepdims=True)
    probs = exponent / row_total
    probs_low = probs.astype(jnp.bfloat16)
    mixed_heads = jnp.einsum(
        "kgqs,skh->qkgh", probs_low, value_low, preferred_element_type=jnp.float32
    )
    attended_low = mixed_heads.reshape(num_rows, D).astype(jnp.bfloat16)
    hidden = inputs + contract_last(attended_low, attention[QKV:])
    normed_two, inv_two = normalize(hidden, gains[1])
    normed_two_low = normed_two.astype(jnp.bfloat16)

    normed_four = four_blocks(normed_two_low)
    gate_proj = contract_last(normed_four, w_gate)
    up_proj = contract_last(normed_four, w_up)
    gate_sigmoid = jax.nn.sigmoid(gate_proj)
    active_low = (gate_proj * gate_sigmoid * up_proj).astype(jnp.bfloat16)
    grad_active = contract_last(upstream_four, w_down)
    grad_gate_low = (
        grad_active * up_proj * gate_sigmoid * (1.0 + gate_proj * (1.0 - gate_sigmoid))
    ).astype(jnp.bfloat16)
    grad_up_low = (grad_active * gate_proj * gate_sigmoid).astype(jnp.bfloat16)
    back_four = plain_dot(grad_gate_low, w_gate) + plain_dot(grad_up_low, w_up)
    back_four, grad_gate_low, grad_up_low, active_low = start_together(
        [back_four, grad_gate_low, grad_up_low, active_low]
    )
    grad_normed_two = back_to_owner(back_four)

    mlp_held = [near_bits[::-1] for _ in range(3)]
    mlp_parts = [
        split_rows(contract_first(left, right).astype(jnp.bfloat16), quarter, mlp_owned)
        for left, right in (
            (grad_gate_low, normed_four),
            (grad_up_low, normed_four),
            (active_low, upstream_four),
        )
    ]

    def mlp_sends(step):
        return [
            take(mlp_parts[i], mlp_held[i].index(orders[i][step]), 1) for i in range(3)
        ]

    def mlp_receive(step, comes):
        for i in range(3):
            bit = orders[i][step]
            kept = take(mlp_parts[i], mlp_held[i].index(bit), 0)
            mlp_held[i].remove(bit)
            mlp_parts[i] = add_low(kept, comes[i], step == steps - 1)

    first_comes = [
        swap(away, size, orders[i][0]) for i, away in enumerate(mlp_sends(0))
    ]

    grad_mid, grad_gain_two = norm_backward(hidden, gains[1], inv_two, grad_normed_two)
    grad_hidden = upstream + grad_mid
    grad_hidden_low = grad_hidden.astype(jnp.bfloat16)
    grad_hidden_low, active_low = start_together([grad_hidden_low, active_low])
    layer_out = (hidden + back_to_owner(plain_dot(active_low, w_down))).astype(jnp.bfloat16)
    grad_out_proj = contract_first(grad_hidden_low, attended_low).astype(jnp.bfloat16)
    grad_attended_low = plain_dot(grad_hidden_low, attention[QKV:]).astype(jnp.bfloat16)
    grad_part = grad_attended_low.reshape(num_rows, KV_HEADS, GROUP, HEAD)
    value_grad = jnp.einsum(
        "kgqs,qkgh->skh", probs_low, grad_part, preferred_element_type=jnp.float32
    )
    grad_probs = jnp.einsum(
        "qkgh,skh->kgqs", grad_part, value_low, preferred_element_type=jnp.float32
    )
    row_inner = jnp.sum(probs * grad_probs, axis=-1, keepdims=True)
    score_grad_low = (probs * (grad_probs - row_inner) * HEAD ** (-0.5)).astype(jnp.bfloat16)
    query_grad = jnp.einsum(
        "kgqs,skh->qkgh", score_grad_low, key_low, preferred_element_type=jnp.float32
    )
    key_grad = jnp.einsum(
        "kgqs,qkgh->skh", score_grad_low, query, preferred_element_type=jnp.float32
    )
    query_pre = unrotate(query_grad.reshape(num_rows, HEADS, HEAD), cosine, sine_table)
    key_pre = unrotate(key_grad, cosine, sine_table)
    grad_qkv_low = jnp.concatenate(
        [
            query_pre.reshape(num_rows, D),
            key_pre.reshape(num_rows, kv_width),
            value_grad.reshape(num_rows, kv_width),
        ],
        axis=1,
    ).astype(jnp.bfloat16)
    grad_qkv_low, *first_comes = start_together([grad_qkv_low] + first_comes)
    grad_bias_term = jnp.sum(grad_qkv_low, axis=0, dtype=jnp.float32)
    grad_qkv_weights = contract_first(grad_qkv_low, normed_low).astype(jnp.bfloat16)
    grad_normed_one = plain_dot(grad_qkv_low, attention[:QKV])
    grad_input_mid, grad_gain_one = norm_backward(inputs, gains[0], inv_one, grad_normed_one)
    grad_tokens = grad_hidden + grad_input_mid

    attn_term = jnp.concatenate([grad_qkv_weights, grad_out_proj], axis=0)
    attn_parts = [
        split_rows(attn_term[:, left:right], size, attn_owned)
        for left, right in zip(edges[:-1], edges[1:])
    ]
    attn_orders = [[0] + order + [top] for order in orders]
    attn_held = [list(range(top, -1, -1)) for _ in range(3)]
    small = jnp.concatenate([grad_gain_one, grad_gain_two, grad_bias_term])
    mlp_receive(0, first_comes)
    for step in range(top + 1):
        sends, keeps = [], []
        for i in range(3):
            bit = attn_orders[i][step]
            axis = attn_held[i].index(bit)
            mine = (index >> bit) & 1
            sends.append(lax.dynamic_index_in_dim(attn_parts[i], 1 - mine, axis, keepdims=False))
            keeps.append(lax.dynamic_index_in_dim(attn_parts[i], mine, axis, keepdims=False))
            attn_held[i].remove(bit)
        sends.append(small)
        if step + 1 < steps:
            sends += mlp_sends(step + 1)
        sends = start_together(sends)
        small = sends[3]
        comes = [swap(sends[i], size, attn_orders[i][step]) for i in range(3)]
        small = small + swap(small, size, step)
        if step + 1 < steps:
            mlp_receive(
                step + 1,
                [swap(sends[4 + i], size, orders[i][step + 1]) for i in range(3)],
            )
        attn_parts = [add_low(keeps[i], comes[i], step == top) for i in range(3)]
    grad_attn = jnp.concatenate(attn_parts, axis=1)
    grad_mlp = jnp.stack(mlp_parts, axis=1)
    grad_gains = small[: 2 * D].reshape(2, D)
    return (layer_out, grad_tokens, grad_attn, grad_mlp, grad_gains, small[2 * D :])


def solution(mesh):
    placed = (
        P("dp", None),
        P("dp", None),
        P("dp", None, None),
        P(),
        P(),
        P("dp", None),
        P("dp", None),
    )
    return jax.shard_map(
        body,
        mesh=mesh,
        in_specs=placed,
        out_specs=(P("dp", None), P("dp", None), P("dp", None), P("dp", None, None), P(), P()),
        check_vma=False,
    )
```

```python
import jax
import jax.numpy as jnp
from jax import lax
from jax.sharding import PartitionSpec as P

HEADS = 14
KV_HEADS = 2
HEAD = 64
SEQS_DEV = 8
D = 896
GROUP = 7
QKV = 1152


epsilon = 1e-06
rope_base = 1000000.0
neg_fill = -1e30


def layout(lengths, slot_count):
    slot_index = jnp.arange(slot_count, dtype=jnp.int32)
    seq_ends = jnp.cumsum(lengths)
    seq_starts = seq_ends - lengths
    filled = seq_ends[SEQS_DEV - 1]
    segment = jnp.sum((slot_index[:, None] >= seq_ends[None, :]).astype(jnp.int32), axis=1)
    starts_all = jnp.concatenate([seq_starts, filled[None]])
    which = segment[:, None] == jnp.arange(SEQS_DEV + 1, dtype=jnp.int32)[None, :]
    start_of = jnp.sum(jnp.where(which, starts_all[None, :], 0), axis=1)
    position = slot_index - start_of
    live = slot_index < filled
    return (segment, position, live)


def half_turn(heads):
    middle = heads.shape[-1] // 2
    return jnp.concatenate([-heads[..., middle:], heads[..., :middle]], axis=-1)


def rope_tables(position):
    index = jnp.arange(HEAD // 2, dtype=jnp.float32)
    freqs = rope_base ** (-2.0 * index / HEAD)
    angles = position.astype(jnp.float32)[:, None] * freqs[None, :]
    angles = jnp.concatenate([angles, angles], axis=1)
    return (jnp.cos(angles), jnp.sin(angles))


def rotate(heads, cosine, sine_table):
    return heads * cosine[:, None, :] + half_turn(heads) * sine_table[:, None, :]


def unrotate(grads, cosine, sine_table):
    return grads * cosine[:, None, :] - half_turn(grads * sine_table[:, None, :])


def normalize(values, gain):
    inv_rms = lax.rsqrt(jnp.mean(values * values, axis=-1, keepdims=True) + epsilon)
    return (values * inv_rms * gain[None, :], inv_rms)


def norm_backward(values, gain, inv_rms, upstream):
    scaled = gain[None, :] * upstream
    gain_grad = jnp.sum(upstream * values * inv_rms, axis=0)
    input_grad = inv_rms * scaled - values * inv_rms**3 * jnp.mean(
        scaled * values, axis=-1, keepdims=True
    )
    return (input_grad, gain_grad)


def contract_last(left, right):
    return lax.dot_general(
        left, right, (((1,), (1,)), ((), ())), preferred_element_type=jnp.float32
    )


def contract_first(left, right):
    return lax.dot_general(
        left, right, (((0,), (0,)), ((), ())), preferred_element_type=jnp.float32
    )


def plain_dot(left, right):
    return jnp.dot(left, right, preferred_element_type=jnp.float32)


def bits_of(size):
    return size.bit_length() - 1


def swap(value, size, bit):
    return lax.ppermute(value, "dp", [(i, i ^ (1 << bit)) for i in range(size)])


def orders_of(bits):
    near, far = bits[:3], bits[3:]
    return tuple(near[i:] + near[:i] + far for i in range(3))


def start_together(values):
    return list(lax.optimization_barrier(tuple(values)))


def take(value, axis, which):
    return lax.index_in_dim(value, which, axis, keepdims=False)


def add_low(kept, come, last):
    total = kept.astype(jnp.float32) + come.astype(jnp.float32)
    return total if last else total.astype(jnp.bfloat16)


def split_rows(value, count, rows):
    return value.reshape((2,) * bits_of(count) + (rows, value.shape[-1]))


def body(tokens, attn_weights, mlp_weights, norm_gains, qkv_bias, seq_lengths, cotangent):
    size = lax.axis_size("dp")
    index = lax.axis_index("dp")
    top = bits_of(size) - 1
    quarter = size // 4
    near_bits = list(range(1, top))
    orders = orders_of(near_bits)
    num_rows = tokens.shape[0]
    attn_owned = attn_weights.shape[0]
    mlp_owned = mlp_weights.shape[0]
    kv_width = KV_HEADS * HEAD

    edges = (0, 384, 640, D)
    attn_parts = [attn_weights[:, left:right] for left, right in zip(edges[:-1], edges[1:])]
    attn_held = [[], [], []]
    pieces = [mlp_weights[:, i, :] for i in range(3)]
    held = [[], [], []]
    steps = len(near_bits)

    def widen_attn(step):
        for i in range(3):
            bit = (orders[i] + [top])[steps - step]
            come = swap(attn_parts[i], size, bit)
            first = ((index >> bit) & 1) == 0
            attn_held[i] = sorted(attn_held[i] + [bit], reverse=True)
            attn_parts[i] = jnp.stack(
                [jnp.where(first, attn_parts[i], come), jnp.where(first, come, attn_parts[i])],
                axis=attn_held[i].index(bit),
            )

    def widen_mlp(step):
        for i in range(3):
            bit = orders[i][steps - 1 - step]
            come = swap(pieces[i], size, bit)
            held[i] = sorted(held[i] + [bit], reverse=True)
            pieces[i] = jnp.stack([pieces[i], come], axis=held[i].index(bit))

    attn_parts = start_together(attn_parts)
    widen_attn(0)
    for step in range(steps):
        together = start_together(attn_parts + pieces)
        attn_parts, pieces = together[:3], together[3:]
        widen_attn(step + 1)
        if step < steps - 1:
            widen_mlp(step)
    attn_half = jnp.concatenate(
        [part.reshape(size // 2, attn_owned, part.shape[-1]) for part in attn_parts], axis=2
    )
    attn_half, cotangent, *pieces = start_together([attn_half, cotangent] + pieces)
    attn_other = swap(attn_half, size, 0)
    last_comes = [swap(pieces[i], size, orders[i][0]) for i in range(3)]
    attention = jnp.stack(
        [
            jnp.where(index & 1 == 0, attn_half, attn_other),
            jnp.where(index & 1 == 0, attn_other, attn_half),
        ],
        axis=1,
    ).reshape(size * attn_owned, D)

    def four_blocks(own):
        far = swap(own, size, top)
        return jnp.concatenate([own, swap(own, size, 0), far, swap(far, size, 0)], axis=0)

    def back_to_owner(partial):
        four = partial.reshape(2, 2, num_rows, D)
        pair = four[:, 0] + swap(four[:, 1], size, 0)
        return pair[0] + swap(pair[1].astype(jnp.bfloat16), size, top).astype(jnp.float32)

    segment, position, live = layout(seq_lengths[0], num_rows)
    slot_index = jnp.arange(num_rows, dtype=jnp.int32)
    gains = norm_gains.astype(jnp.float32)
    biases = qkv_bias.astype(jnp.float32)
    inputs = tokens.astype(jnp.float32)
    upstream = cotangent.astype(jnp.float32) * live.astype(jnp.float32)[:, None]
    upstream_low = upstream.astype(jnp.bfloat16)
    upstream_four = four_blocks(upstream_low)

    normed_one, inv_one = normalize(inputs, gains[0])
    normed_low = normed_one.astype(jnp.bfloat16)
    projected = contract_last(normed_low, attention[:QKV]) + biases[None, :]
    cosine, sine_table = rope_tables(position)
    query_low = rotate(projected[:, :D].reshape(num_rows, HEADS, HEAD), cosine, sine_table).astype(
        jnp.bfloat16
    )
    key_low = rotate(
        projected[:, D : D + kv_width].reshape(num_rows, KV_HEADS, HEAD), cosine, sine_table
    ).astype(jnp.bfloat16)
    value_low = projected[:, D + kv_width :].reshape(num_rows, KV_HEADS, HEAD).astype(jnp.bfloat16)
    query_low, *last_comes = start_together([query_low] + last_comes)
    w_gate, w_up, w_down = [
        jnp.stack([pieces[i], last_comes[i]], axis=near_bits[::-1].index(orders[i][0])).reshape(
            quarter * mlp_owned, D
        )
        for i in range(3)
    ]
    query = query_low.reshape(num_rows, KV_HEADS, GROUP, HEAD)
    allowed = (segment[:, None] == segment[None, :]) & (slot_index[None, :] <= slot_index[:, None])
    raw_scores = jnp.einsum("qkgh,skh->kgqs", query, key_low, preferred_element_type=jnp.float32)
    scores = jnp.where(allowed[None, None], raw_scores * HEAD ** (-0.5), neg_fill)
    row_peak = jnp.max(scores, axis=-1, keepdims=True)
    exponent = jnp.exp(scores - row_peak)
    row_total = jnp.sum(exponent, axis=-1, keepdims=True)
    probs = exponent / row_total
    probs_low = probs.astype(jnp.bfloat16)
    mixed_heads = jnp.einsum(
        "kgqs,skh->qkgh", probs_low, value_low, preferred_element_type=jnp.float32
    )
    attended_low = mixed_heads.reshape(num_rows, D).astype(jnp.bfloat16)
    hidden = inputs + contract_last(attended_low, attention[QKV:])
    normed_two, inv_two = normalize(hidden, gains[1])
    normed_two_low = normed_two.astype(jnp.bfloat16)

    normed_four = four_blocks(normed_two_low)
    gate_proj = contract_last(normed_four, w_gate)
    up_proj = contract_last(normed_four, w_up)
    gate_sigmoid = jax.nn.sigmoid(gate_proj)
    active_low = (gate_proj * gate_sigmoid * up_proj).astype(jnp.bfloat16)
    grad_active = contract_last(upstream_four, w_down)
    grad_gate_low = (
        grad_active * up_proj * gate_sigmoid * (1.0 + gate_proj * (1.0 - gate_sigmoid))
    ).astype(jnp.bfloat16)
    grad_up_low = (grad_active * gate_proj * gate_sigmoid).astype(jnp.bfloat16)
    back_four = plain_dot(grad_gate_low, w_gate) + plain_dot(grad_up_low, w_up)
    back_four, grad_gate_low, grad_up_low, active_low = start_together(
        [back_four, grad_gate_low, grad_up_low, active_low]
    )
    grad_normed_two = back_to_owner(back_four)

    mlp_held = [near_bits[::-1] for _ in range(3)]
    mlp_parts = [
        split_rows(contract_first(left, right).astype(jnp.bfloat16), quarter, mlp_owned)
        for left, right in (
            (grad_gate_low, normed_four),
            (grad_up_low, normed_four),
            (active_low, upstream_four),
        )
    ]

    def mlp_sends(step):
        return [
            take(mlp_parts[i], mlp_held[i].index(orders[i][step]), 1) for i in range(3)
        ]

    def mlp_receive(step, comes):
        for i in range(3):
            bit = orders[i][step]
            kept = take(mlp_parts[i], mlp_held[i].index(bit), 0)
            mlp_held[i].remove(bit)
            mlp_parts[i] = add_low(kept, comes[i], step == steps - 1)

    first_comes = [
        swap(away, size, orders[i][0]) for i, away in enumerate(mlp_sends(0))
    ]

    grad_mid, grad_gain_two = norm_backward(hidden, gains[1], inv_two, grad_normed_two)
    grad_hidden = upstream + grad_mid
    grad_hidden_low = grad_hidden.astype(jnp.bfloat16)
    grad_hidden_low, active_low = start_together([grad_hidden_low, active_low])
    layer_out = (hidden + back_to_owner(plain_dot(active_low, w_down))).astype(jnp.bfloat16)
    grad_out_proj = contract_first(grad_hidden_low, attended_low).astype(jnp.bfloat16)
    grad_attended_low = plain_dot(grad_hidden_low, attention[QKV:]).astype(jnp.bfloat16)
    grad_part = grad_attended_low.reshape(num_rows, KV_HEADS, GROUP, HEAD)
    value_grad = jnp.einsum(
        "kgqs,qkgh->skh", probs_low, grad_part, preferred_element_type=jnp.float32
    )
    grad_probs = jnp.einsum(
        "qkgh,skh->kgqs", grad_part, value_low, preferred_element_type=jnp.float32
    )
    row_inner = jnp.sum(probs * grad_probs, axis=-1, keepdims=True)
    score_grad_low = (probs * (grad_probs - row_inner) * HEAD ** (-0.5)).astype(jnp.bfloat16)
    query_grad = jnp.einsum(
        "kgqs,skh->qkgh", score_grad_low, key_low, preferred_element_type=jnp.float32
    )
    key_grad = jnp.einsum(
        "kgqs,qkgh->skh", score_grad_low, query, preferred_element_type=jnp.float32
    )
    query_pre = unrotate(query_grad.reshape(num_rows, HEADS, HEAD), cosine, sine_table)
    key_pre = unrotate(key_grad, cosine, sine_table)
    grad_qkv_low = jnp.concatenate(
        [
            query_pre.reshape(num_rows, D),
            key_pre.reshape(num_rows, kv_width),
            value_grad.reshape(num_rows, kv_width),
        ],
        axis=1,
    ).astype(jnp.bfloat16)
    grad_qkv_low, layer_out, *first_comes = start_together(
        [grad_qkv_low, layer_out] + first_comes
    )
    grad_bias_term = jnp.sum(grad_qkv_low, axis=0, dtype=jnp.float32)
    grad_qkv_weights = contract_first(grad_qkv_low, normed_low).astype(jnp.bfloat16)
    grad_normed_one = plain_dot(grad_qkv_low, attention[:QKV])
    grad_input_mid, grad_gain_one = norm_backward(inputs, gains[0], inv_one, grad_normed_one)
    grad_tokens = grad_hidden + grad_input_mid

    attn_term = jnp.concatenate([grad_qkv_weights, grad_out_proj], axis=0)
    attn_parts = [
        split_rows(attn_term[:, left:right], size, attn_owned)
        for left, right in zip(edges[:-1], edges[1:])
    ]
    attn_orders = [[0] + order + [top] for order in orders]
    attn_held = [list(range(top, -1, -1)) for _ in range(3)]
    small = jnp.concatenate([grad_gain_one, grad_gain_two, grad_bias_term])
    mlp_receive(0, first_comes)
    for step in range(top + 1):
        sends, keeps = [], []
        for i in range(3):
            bit = attn_orders[i][step]
            axis = attn_held[i].index(bit)
            mine = (index >> bit) & 1
            sends.append(lax.dynamic_index_in_dim(attn_parts[i], 1 - mine, axis, keepdims=False))
            keeps.append(lax.dynamic_index_in_dim(attn_parts[i], mine, axis, keepdims=False))
            attn_held[i].remove(bit)
        sends.append(small)
        if step + 1 < steps:
            sends += mlp_sends(step + 1)
        sends = start_together(sends)
        small = sends[3]
        comes = [swap(sends[i], size, attn_orders[i][step]) for i in range(3)]
        small = small + swap(small, size, step)
        if step + 1 < steps:
            mlp_receive(
                step + 1,
                [swap(sends[4 + i], size, orders[i][step + 1]) for i in range(3)],
            )
        attn_parts = [add_low(keeps[i], comes[i], step == top) for i in range(3)]
    grad_attn = jnp.concatenate(attn_parts, axis=1)
    grad_mlp = jnp.stack(mlp_parts, axis=1)
    grad_gains = small[: 2 * D].reshape(2, D)
    return (layer_out, grad_tokens, grad_attn, grad_mlp, grad_gains, small[2 * D :])


def solution(mesh):
    placed = (
        P("dp", None),
        P("dp", None),
        P("dp", None, None),
        P(),
        P(),
        P("dp", None),
        P("dp", None),
    )
    return jax.shard_map(
        body,
        mesh=mesh,
        in_specs=placed,
        out_specs=(P("dp", None), P("dp", None), P("dp", None), P("dp", None, None), P(), P()),
        check_vma=False,
    )
```
